32 devices in a mesh: groups: 2 (over y), tensor: 4 (over z), adapter: 4 (over x, core).
Axes of the slice: x: 2, y: 2, z: 4, core: 2. Of those that a mesh axis runs over, the one named last changes fastest.
Arguments:
- attended: bfloat16 [8, 64, 8192], P(('groups', 'adapter'), None, 'tensor'), parts along dimension 0, may hold values from -6 to 6
- out_weight: bfloat16 [8192, 8192], P('tensor'), may hold values from -0.0625 to 0.0625
- adapter_ids: int32 [8, 64], P(('groups', 'adapter')), parts along dimension 0, may hold values from 0 to 127, as said below
- shrink_weight: bfloat16 [128, 8192, 64], P('adapter', 'tensor'), may hold values from -0.0625 to 0.0625
- expand_weight: bfloat16 [128, 64, 8192], P('adapter', None, 'tensor'), may hold values from -0.75 to 0.75
Outputs:
- projected: bfloat16 [8, 64, 8192], P(('groups', 'adapter'), 'tensor'), parts along dimension 0
The draws below stay inside these ranges and needn't reach their ends.
There are 2 independent parts, one for each index of `groups`. The reference program is written for one: setup_inputs(seed, part) draws one part's arguments, and reference() takes and returns one part's arrays. A program takes and returns all parts, laid end to end along the dimension named above; an argument that names none is the same for every part. Nothing has to cross between parts.
Inputs may be any that keep to these rules, and one draw needn't show every extreme that they name: `adapter_ids`: adapter j belongs to owner j // 32. In every block b, at most 32 rows use adapters of one owner, and exactly 32 rows use adapters of one owner, the same owner for every block.
All inputs are finite; a program needn't handle non-finite values.
Results may differ from the reference program's by a relative error of at most 0.013.
Values may be sent and summed in bfloat16 or wider, within the bound.
A program may use at most 128 MiB of HBM per device.

```python
import jax
import jax.numpy as jnp
from jax import lax

D = 8192
RANK = 64
ROWS_DEV = 16
ADP_DEV = 32
OWNERS = 4
RA = 64
CAP = 32
NADP = 128
N_TENSOR = 4


def draw_adapter_ids(key, part):
    key = jax.random.fold_in(key, 11)
    key_hot, key_perm, key_other, key_first, key_second, key_shift = jax.random.split(key, 6)
    owner_count = NADP // ADP_DEV
    hot_owner = jax.random.randint(key_hot, (), 0, owner_count)
    perm_keys = jax.random.split(key_perm, owner_count)
    shuffled = jax.vmap(lambda one_key: jax.random.permutation(one_key, RA))(perm_keys)
    is_hot = shuffled < CAP
    other_owner = (hot_owner + 1 + jax.random.randint(key_other, (owner_count, RA), 0, owner_count - 1)) % owner_count
    owning_adapter = jnp.where(is_hot, hot_owner, other_owner)
    first_pick = jax.random.randint(key_first, (owner_count, RA), 0, ADP_DEV)
    second_pick = jax.random.randint(key_second, (owner_count, RA), 0, ADP_DEV)
    shift_by = jax.random.randint(key_shift, (owner_count, 1), 0, ADP_DEV)
    local_slot = (jnp.minimum(first_pick, second_pick) + shift_by) % ADP_DEV
    return (owning_adapter * ADP_DEV + local_slot).astype(jnp.int32)


def block_levels(rng, shape, cuts, low, largest):
    loudness = 1.0
    for position, parts in cuts:
        draws = jax.random.uniform(jax.random.fold_in(jax.random.fold_in(rng, 6), position), (parts,), jnp.float32, low / len(cuts), largest / len(cuts))
        loudness = loudness * jnp.repeat(jnp.exp(draws), shape[position] // parts).reshape((-1,) + (1,) * (len(shape) - 1 - position))
    return loudness


def noise(key, extent, spread, most, cuts=(), kind=jnp.bfloat16):
    entries = spread * jax.random.normal(key, extent, jnp.float32)
    if cuts:
        entries = entries * block_levels(key, extent, cuts, -0.22, 0.18)
    return jnp.clip(entries, -most, most).astype(kind)


def setup_inputs(seed: int = 0, part: int = 0) -> dict:
    key_list = jax.random.split(jax.random.key(seed), 6)
    own_keys = jax.random.split(jax.random.fold_in(key_list[5], part), 6)
    return {
        "attended": noise(own_keys[0], (OWNERS, RA, D), 1.0, 6.0, ((0, 4), (2, 4))),
        "out_weight": noise(key_list[1], (D, D), D ** -0.5, 0.0625, ((0, 4),)),
        "adapter_ids": draw_adapter_ids(jax.random.fold_in(jax.random.fold_in(key_list[5], part), 71), part),
        "shrink_weight": noise(key_list[3], (NADP, D, RANK), D ** -0.5, 0.0625, ((0, 4), (1, 4))),
        "expand_weight": noise(key_list[4], (NADP, RANK, D), RANK ** -0.5, 0.75, ((0, 4), (2, 4))),
    }


ADAPTER_SCALING = 0.5


def reference(attended, out_weight, adapter_ids, shrink_weight, expand_weight):
    flat_rows = attended.reshape(-1, D)
    slice_width = D // N_TENSOR
    row_slices = jnp.transpose(flat_rows.reshape(-1, N_TENSOR, slice_width), (1, 0, 2))
    weight_slices = out_weight.reshape(N_TENSOR, slice_width, D)

    def add_partial(total, pair):
        row_portion, weight_part = pair
        partial_value = jnp.dot(row_portion, weight_part, preferred_element_type=jnp.float32).astype(jnp.bfloat16)
        return total + partial_value.astype(jnp.float32), None

    base_sum, unused = lax.scan(add_partial, jnp.zeros((flat_rows.shape[0], D), jnp.float32), (row_slices, weight_slices))
    block_rows = flat_rows.reshape(-1, ROWS_DEV, D)
    block_ids = adapter_ids.reshape(-1, ROWS_DEV).astype(jnp.int32)

    def correct(pair):
        rows_here, ids_here = pair
        first_rows = shrink_weight[ids_here].astype(jnp.float32)
        reduced_rank_input = jnp.einsum("bd,bdr->br", rows_here.astype(jnp.float32), first_rows).astype(jnp.bfloat16)
        later_rows = expand_weight[ids_here].astype(jnp.float32)
        return (ADAPTER_SCALING * jnp.einsum("zt,ztq->zq", reduced_rank_input.astype(jnp.float32), later_rows)).astype(jnp.bfloat16)

    correction = lax.map(correct, (block_rows, block_ids)).reshape(-1, D)
    projected = (base_sum + correction.astype(jnp.float32)).astype(jnp.bfloat16)
    return projected.reshape(OWNERS, RA, D)
```

```python
import functools

import jax
import jax.numpy as jnp
from jax import lax
from jax.experimental import pallas as pl
from jax.experimental.pallas import tpu as pltpu
from jax.sharding import PartitionSpec as P

ADAPTER_SCALING = 0.5
MESH = pl.DeviceIdType.MESH
TILE = 256
VMEM_LIMIT = 60 * 2**20
F32 = jnp.float32
BF16 = jnp.bfloat16


def fused_kernel(
    owners, tensors, base_chunks, expand_chunks,
    ids_ref, att_hbm, w_hbm, s_hbm, e_hbm, out_ref,
    att, w, s, e, slots, slot_ids, got, got_ids, home_hot,
    part, part_in, low, low_in, spread, corr, ret, home, home_in,
    att_sem, w_sem, s_sem, e_sem,
    rows_send, rows_recv, ids_send, ids_recv, low_send, low_recv,
    part_send, part_recv, corr_send, corr_recv, home_send, home_recv,
):
    rows, features = att.shape
    width = w.shape[1]
    low_width, slice_width = e.shape
    lanes = slot_ids.shape[1]
    capacity = rows // 2
    n_slots = owners * capacity
    rows_dev = rows // tensors
    rank = lanes // 2
    adapters = low_width // rank
    chunk = width // base_chunks
    piece = slice_width // expand_chunks
    halves = s_sem.shape[0]
    half = low_width // halves
    me = lax.axis_index("adapter")
    plane = lax.axis_index("tensor")

    def load_w(c):
        cols = pl.ds(c * chunk, chunk)
        return pltpu.make_async_copy(w_hbm.at[:, cols], w.at[:, cols], w_sem.at[c])

    def load_s(h):
        some = pl.ds(h * half, half)
        return pltpu.make_async_copy(s_hbm.at[some], s.at[some], s_sem.at[h])

    def load_e(c):
        cols = pl.ds(c * piece, piece)
        return pltpu.make_async_copy(e_hbm.at[:, cols], e.at[:, cols], e_sem.at[c])

    load_att = pltpu.make_async_copy(att_hbm, att, att_sem)
    load_att.start()
    load_w(0).start()
    for h in range(halves):
        load_s(h).start()
    load_w(1).start()

    barrier = pltpu.get_barrier_semaphore()
    for j in range(1, owners):
        pl.semaphore_signal(barrier, inc=1, device_id={"adapter": lax.rem(me + j, owners)}, device_id_type=MESH)
    for j in range(1, tensors):
        pl.semaphore_signal(barrier, inc=1, device_id={"tensor": lax.rem(plane + j, tensors)}, device_id_type=MESH)

    ids = ids_ref[...]
    relative = lax.rem(lax.div(ids, adapters) - me + owners, owners)
    below = lax.broadcasted_iota(jnp.int32, (rows, rows), 0)
    along = lax.broadcasted_iota(jnp.int32, (rows, rows), 1)

    def as_column(row):
        return jnp.sum(jnp.where(below == along, row, 0), axis=1, keepdims=True)

    same = as_column(relative) == relative
    running = jnp.sum(jnp.where(same & (below < along), 1, 0), axis=0, keepdims=True)
    slot_of = relative * capacity + running
    hot = lax.broadcasted_iota(jnp.int32, (n_slots, rows), 0) == slot_of
    home_hot[...] = jnp.where(
        lax.broadcasted_iota(jnp.int32, (rows, n_slots), 1) == as_column(slot_of), 1.0, 0.0
    ).astype(BF16)
    local_slot = jnp.sum(jnp.where(hot, lax.rem(ids, adapters) + 1, 0), axis=1, keepdims=True) - 1
    slot_ids[...] = jnp.broadcast_to(local_slot, (n_slots, lanes))
    load_att.wait()
    hot = jnp.where(hot, 1.0, 0.0).astype(BF16)

    @pl.loop(0, features // TILE)
    def _(i):
        cols = pl.ds(pl.multiple_of(i * TILE, TILE), TILE)
        slots[:, cols] = jnp.dot(hot, att[:, cols], preferred_element_type=F32).astype(BF16)

    pl.semaphore_wait(barrier, owners - 1 + tensors - 1)

    def send_rows(j):
        mine = pl.ds(j * capacity, capacity)
        to = {"adapter": lax.rem(me + j, owners)}
        return (
            pltpu.make_async_remote_copy(
                src_ref=slots.at[mine], dst_ref=got.at[mine],
                send_sem=rows_send.at[j - 1], recv_sem=rows_recv.at[j - 1],
                device_id=to, device_id_type=MESH,
            ),
            pltpu.make_async_remote_copy(
                src_ref=slot_ids.at[mine], dst_ref=got_ids.at[mine],
                send_sem=ids_send.at[j - 1], recv_sem=ids_recv.at[j - 1],
                device_id=to, device_id_type=MESH,
            ),
        )

    def send_part(j, c):
        cols = pl.ds(c * chunk, chunk)
        to = lax.rem(plane + j, tensors)
        return pltpu.make_async_remote_copy(
            src_ref=part.at[to, :, cols], dst_ref=part_in.at[j - 1, :, cols],
            send_sem=part_send.at[j - 1, c], recv_sem=part_recv.at[j - 1, c],
            device_id={"tensor": to}, device_id_type=MESH,
        )

    def send_low(j):
        return pltpu.make_async_remote_copy(
            src_ref=low, dst_ref=low_in.at[j - 1],
            send_sem=low_send.at[j - 1], recv_sem=low_recv.at[j - 1],
            device_id={"tensor": lax.rem(plane + j, tensors)}, device_id_type=MESH,
        )

    def send_corr(j, c):
        mine, cols = pl.ds(j * capacity, capacity), pl.ds(c * piece, piece)
        return pltpu.make_async_remote_copy(
            src_ref=corr.at[mine, cols], dst_ref=ret.at[mine, cols],
            send_sem=corr_send.at[j - 1, c], recv_sem=corr_recv.at[j - 1, c],
            device_id={"adapter": lax.rem(me - j + owners, owners)}, device_id_type=MESH,
        )

    def send_home(j, c):
        cols = pl.ds(c * piece, piece)
        to = lax.rem(plane + j, tensors)
        return pltpu.make_async_remote_copy(
            src_ref=home.at[to, :, cols], dst_ref=home_in.at[j - 1, :, cols],
            send_sem=home_send.at[j - 1, c], recv_sem=home_recv.at[j - 1, c],
            device_id={"tensor": to}, device_id_type=MESH,
        )

    for j in range(1, owners):
        for copy in send_rows(j):
            copy.start()
    got[pl.ds(0, capacity)] = slots[pl.ds(0, capacity)]
    got_ids[pl.ds(0, capacity)] = slot_ids[pl.ds(0, capacity)]

    def base(c):
        if c + 2 < base_chunks:
            load_w(c + 2).start()
        load_w(c).wait()

        @pl.loop(0, chunk // TILE)
        def _(i):
            cols = pl.ds(pl.multiple_of(c * chunk + i * TILE, TILE), TILE)
            product = jnp.dot(att[...], w[:, cols], preferred_element_type=F32).astype(BF16)
            for to in range(tensors):
                part[to, :, cols] = product[to * rows_dev:(to + 1) * rows_dev]

        for j in range(1, tensors):
            send_part(j, c).start()

    def shrink():
        for j in range(1, owners):
            for copy in send_rows(j):
                copy.wait_recv()
        for h in range(halves):
            load_s(h).wait()
        lane_parity = lax.div(lax.broadcasted_iota(jnp.int32, (n_slots, lanes), 1), rank)
        wanted = got_ids[...] - lane_parity

        def step(i, total):
            some = pl.ds(pl.multiple_of(i * TILE, TILE), TILE)
            products = lax.dot_general(
                got[...], s[some, :], (((1,), (1,)), ((), ())), preferred_element_type=F32
            )
            for k in range(TILE // lanes):
                here = products[:, k * lanes:(k + 1) * lanes]
                total += jnp.where(wanted == 2 * (i * (TILE // lanes) + k), here, 0.0)
            return total

        total = lax.fori_loop(0, low_width // TILE, step, jnp.zeros((n_slots, lanes), F32))
        low[...] = total.astype(BF16)
        for j in range(1, tensors):
            send_low(j).start()

    def expand():
        shrunk = low[...].astype(F32)
        for j in range(1, tensors):
            send_low(j).wait_recv()
            shrunk += low_in[j - 1].astype(F32)
        pair = lax.shift_right_arithmetic(got_ids[...], 1)
        for p in range(low_width // lanes):
            spread[:, p * lanes:(p + 1) * lanes] = jnp.where(pair == p, shrunk, 0.0).astype(BF16)
        for c in range(expand_chunks):
            load_e(c).wait()

            @pl.loop(0, piece // TILE)
            def _(i):
                cols = pl.ds(pl.multiple_of(c * piece + i * TILE, TILE), TILE)
                corr[:, cols] = (
                    ADAPTER_SCALING * jnp.dot(spread[...], e[:, cols], preferred_element_type=F32)
                ).astype(BF16)

            for j in range(1, owners):
                send_corr(j, c).start()
        ret[pl.ds(0, capacity)] = corr[pl.ds(0, capacity)]

    def merge(c):
        for j in range(1, owners):
            send_corr(j, c).wait_recv()
        cols = pl.ds(c * piece, piece)
        merged = jnp.dot(home_hot[...], ret[:, cols], preferred_element_type=F32).astype(BF16)
        for to in range(tensors):
            home[to, :, cols] = merged[to * rows_dev:(to + 1) * rows_dev]
        for j in range(1, tensors):
            send_home(j, c).start()

    base(0)
    base(1)
    for c in range(expand_chunks):
        load_e(c).start()
    base(2)
    shrink()
    base(3)
    base(4)
    expand()
    for c in range(5, base_chunks):
        base(c)
    for c in range(expand_chunks):
        merge(c)

    for c in range(base_chunks):
        cols = pl.ds(c * chunk, chunk)
        total = part[plane, :, cols].astype(F32)
        for j in range(1, tensors):
            send_part(j, c).wait_recv()
            total += part_in[j - 1, :, cols].astype(F32)
        out_ref[:, cols] = total
    for j in range(tensors):
        for c in range(expand_chunks):
            if j:
                send_home(j, c).wait_recv()
        source = lax.rem(plane - j + tensors, tensors)
        cols = pl.ds(pl.multiple_of(source * slice_width, slice_width), slice_width)
        own = home_in[j - 1] if j else home[plane]
        out_ref[:, cols] += own.astype(F32)

    for j in range(1, owners):
        for copy in send_rows(j):
            copy.wait_send()
        for c in range(expand_chunks):
            send_corr(j, c).wait_send()
    for j in range(1, tensors):
        send_low(j).wait_send()
        for c in range(base_chunks):
            send_part(j, c).wait_send()
        for c in range(expand_chunks):
            send_home(j, c).wait_send()


def fused(attended, out_weight, adapter_ids, shrink_weight, expand_weight):
    owners, tensors = lax.axis_size("adapter"), lax.axis_size("tensor")
    rows, features = attended.shape[1:]
    width = out_weight.shape[1]
    adapters, rank, slice_width = expand_weight.shape
    low_width, lanes = adapters * rank, 2 * rank
    n_slots, rows_dev = owners * (rows // 2), rows // tensors
    base_chunks, expand_chunks, halves = 8, 4, 2
    dma = lambda *shape: pltpu.SemaphoreType.DMA(shape)
    pairs = lambda n: [dma(n), dma(n)]
    grids = lambda n, m: [dma(n, m), dma(n, m)]
    vmem = lambda *shape: pltpu.VMEM(shape, BF16)
    ints = lambda *shape: pltpu.VMEM(shape, jnp.int32)
    summed = pl.pallas_call(
        functools.partial(fused_kernel, owners, tensors, base_chunks, expand_chunks),
        out_shape=jax.ShapeDtypeStruct((rows_dev, width), F32),
        in_specs=[pl.BlockSpec(memory_space=pltpu.VMEM)] + [pl.BlockSpec(memory_space=pl.ANY)] * 4,
        out_specs=pl.BlockSpec(memory_space=pltpu.VMEM),
        scratch_shapes=[
            vmem(rows, features),
            vmem(features, width),
            vmem(low_width, features),
            vmem(low_width, slice_width),
            vmem(n_slots, features),
            ints(n_slots, lanes),
            vmem(n_slots, features),
            ints(n_slots, lanes),
            vmem(rows, n_slots),
            vmem(tensors, rows_dev, width),
            vmem(tensors - 1, rows_dev, width),
            vmem(n_slots, lanes),
            vmem(tensors - 1, n_slots, lanes),
            vmem(n_slots, low_width),
            vmem(n_slots, slice_width),
            vmem(n_slots, slice_width),
            vmem(tensors, rows_dev, slice_width),
            vmem(tensors - 1, rows_dev, slice_width),
            pltpu.SemaphoreType.DMA,
            dma(base_chunks),
            dma(halves),
            dma(expand_chunks),
            *pairs(owners - 1),
            *pairs(owners - 1),
            *pairs(tensors - 1),
            *grids(tensors - 1, base_chunks),
            *grids(owners - 1, expand_chunks),
            *grids(tensors - 1, expand_chunks),
        ],
        compiler_params=pltpu.CompilerParams(
            collective_id=0, has_side_effects=True, vmem_limit_bytes=VMEM_LIMIT
        ),
    )(
        adapter_ids,
        attended[0],
        out_weight,
        jnp.swapaxes(shrink_weight, 1, 2).reshape(low_width, features),
        expand_weight.reshape(low_width, slice_width),
    )
    return summed.astype(BF16)[None]


def fits(attended, out_weight, shrink_weight, expand_weight):
    owners, tensors = lax.axis_size("adapter"), lax.axis_size("tensor")
    rows, features = attended.shape[1:]
    width, slice_width = out_weight.shape[1], expand_weight.shape[2]
    low_width = expand_weight.shape[0] * expand_weight.shape[1]
    slots = owners * (rows // 2)
    values = out_weight.size + shrink_weight.size + expand_weight.size
    values += rows * (features + 4 * width) + slots * (2 * features + low_width + 3 * slice_width)
    tiled = rows % (16 * tensors) == 0 and width % (8 * TILE) == 0 and slice_width % (4 * TILE) == 0
    return tiled and features % TILE == 0 and 2 * values <= VMEM_LIMIT


def plain(attended, out_weight, adapter_ids, shrink_weight, expand_weight):
    inputs = attended[0]
    rows_all, features = inputs.shape
    owners = lax.axis_size("adapter")
    adapters_dev = shrink_weight.shape[0]
    capacity = rows_all // 2
    row_ids = adapter_ids[0]
    owning_adapter = row_ids // adapters_dev
    local_slot = row_ids % adapters_dev
    owner_hot = (owning_adapter[:, None] == jnp.arange(owners)[None, :]).astype(jnp.int32)
    running = jnp.cumsum(owner_hot, axis=0) - 1
    slot_of = owning_adapter * capacity + jnp.sum(running * owner_hot, axis=1)
    slot_ids = jnp.full((owners * capacity,), -1, jnp.int32).at[slot_of].set(local_slot)
    outgoing = jnp.zeros((owners * capacity, features), jnp.bfloat16).at[slot_of].set(inputs)
    recv_rows, recv_ids = (
        lax.all_to_all(outgoing, "adapter", split_axis=0, concat_axis=0, tiled=True),
        lax.all_to_all(slot_ids, "adapter", split_axis=0, concat_axis=0, tiled=True),
    )
    chosen = (recv_ids[:, None] == jnp.arange(adapters_dev)[None, :]).astype(jnp.float32)
    products = jnp.einsum(
        "nd,adr->nar", recv_rows, shrink_weight, preferred_element_type=jnp.float32
    )
    partial_sum = jnp.sum(products * chosen[:, :, None], axis=1)
    incoming_rows = lax.psum(partial_sum.astype(jnp.bfloat16), "tensor")
    spread = incoming_rows[:, None, :] * chosen.astype(jnp.bfloat16)[:, :, None]
    delta_rows = (
        ADAPTER_SCALING
        * jnp.einsum("nar,ard->nd", spread, expand_weight, preferred_element_type=jnp.float32)
    ).astype(jnp.bfloat16)
    returned = lax.all_to_all(delta_rows, "adapter", split_axis=0, concat_axis=0, tiled=True)
    home_delta = returned[slot_of]
    summed = lax.psum_scatter(
        jnp.dot(inputs, out_weight, preferred_element_type=jnp.float32).astype(jnp.bfloat16),
        "tensor",
        scatter_dimension=0,
        tiled=True,
    ).astype(jnp.float32)
    own_delta = lax.all_to_all(home_delta, "tensor", split_axis=0, concat_axis=1, tiled=True)
    projected = (summed + own_delta.astype(jnp.float32)).astype(jnp.bfloat16)
    return projected[None]


def per_device(attended, out_weight, adapter_ids, shrink_weight, expand_weight):
    form = fused if fits(attended, out_weight, shrink_weight, expand_weight) else plain
    return form(attended, out_weight, adapter_ids, shrink_weight, expand_weight)


def solution(mesh):
    return jax.shard_map(
        per_device,
        mesh=mesh,
        in_specs=(
            P(("groups", "adapter"), None, "tensor"),
            P("tensor", None),
            P(("groups", "adapter"), None),
            P("adapter", "tensor", None),
            P("adapter", None, "tensor"),
        ),
        out_specs=P(("groups", "adapter"), "tensor", None),
        check_vma=False,
    )
```

```python
import functools

import jax
import jax.numpy as jnp
from jax import lax
from jax.experimental import pallas as pl
from jax.experimental.pallas import tpu as pltpu
from jax.sharding import PartitionSpec as P

ADAPTER_SCALING = 0.5
MESH = pl.DeviceIdType.MESH
TILE = 256
BASE_TILE = 512
WIDE = 2048
EARLY = 0
VMEM_LIMIT = 60 * 2**20
F32 = jnp.float32
BF16 = jnp.bfloat16


def fused_kernel(
    owners, tensors, base_chunks, expand_chunks, row_chunks,
    ids_ref, att_hbm, w_hbm, s_hbm, e_hbm, out_ref,
    att, w, s, e, slots, slot_ids, got, got_ids, home_hot,
    part, pair_in, cross, cross_in, low, low_in, spread, corr, ret, home, home_in,
    att_sem, w_sem, s_sem, e_sem,
    rows_send, rows_recv, ids_send, ids_recv, low_send, low_recv,
    pair_send, pair_recv, cross_send, cross_recv, corr_send, corr_recv, home_send, home_recv,
):
    rows, features = att.shape
    width = w.shape[1]
    low_width, slice_width = e.shape
    lanes = slot_ids.shape[1]
    capacity = rows // 2
    n_slots = owners * capacity
    rows_dev = rows // tensors
    rank = lanes // 2
    adapters = low_width // rank
    chunk = width // base_chunks
    piece = slice_width // expand_chunks
    strip = features // row_chunks
    me = lax.axis_index("adapter")
    plane = lax.axis_index("tensor")
    partner = plane + 1 - 2 * lax.rem(plane, 2)
    across = lax.rem(plane + 2, tensors)
    partner_across = lax.rem(partner + 2, tensors)

    def load_w(c):
        cols = pl.ds(c * chunk, chunk)
        return pltpu.make_async_copy(w_hbm.at[:, cols], w.at[:, cols], w_sem.at[c])

    def load_s(k):
        cols = pl.ds(k * strip, strip)
        return pltpu.make_async_copy(s_hbm.at[:, cols], s.at[:, cols], s_sem.at[k])

    def load_e(c):
        cols = pl.ds(c * piece, piece)
        return pltpu.make_async_copy(e_hbm.at[:, cols], e.at[:, cols], e_sem.at[c])

    load_att = pltpu.make_async_copy(att_hbm, att, att_sem)
    load_att.start()
    for c in range(EARLY):
        load_w(c).start()
    for k in range(row_chunks):
        load_s(k).start()
    for c in range(EARLY, EARLY + 2):
        load_w(c).start()

    barrier = pltpu.get_barrier_semaphore()
    for j in range(1, owners):
        pl.semaphore_signal(barrier, inc=1, device_id={"adapter": lax.rem(me + j, owners)}, device_id_type=MESH)
    for j in range(1, tensors):
        pl.semaphore_signal(barrier, inc=1, device_id={"tensor": lax.rem(plane + j, tensors)}, device_id_type=MESH)

    ids = ids_ref[...]
    relative = lax.rem(lax.div(ids, adapters) - me + owners, owners)
    below = lax.broadcasted_iota(jnp.int32, (rows, rows), 0)
    along = lax.broadcasted_iota(jnp.int32, (rows, rows), 1)

    def as_column(row):
        return jnp.sum(jnp.where(below == along, row, 0), axis=1, keepdims=True)

    same = as_column(relative) == relative
    running = jnp.sum(jnp.where(same & (below < along), 1, 0), axis=0, keepdims=True)
    slot_of = relative * capacity + running
    hot = lax.broadcasted_iota(jnp.int32, (n_slots, rows), 0) == slot_of
    home_hot[...] = jnp.where(
        lax.broadcasted_iota(jnp.int32, (rows, n_slots), 1) == as_column(slot_of), 1.0, 0.0
    ).astype(BF16)
    local_slot = jnp.sum(jnp.where(hot, lax.rem(ids, adapters) + 1, 0), axis=1, keepdims=True) - 1
    slot_ids[...] = jnp.broadcast_to(local_slot, (n_slots, lanes))
    load_att.wait()
    hot = jnp.where(hot, 1.0, 0.0).astype(BF16)

    @pl.loop(0, features // TILE)
    def _(i):
        cols = pl.ds(pl.multiple_of(i * TILE, TILE), TILE)
        slots[:, cols] = jnp.dot(hot, att[:, cols], preferred_element_type=F32).astype(BF16)

    def compute_base(c):
        load_w(c).wait()

        @pl.loop(0, chunk // BASE_TILE)
        def _(i):
            cols = pl.ds(pl.multiple_of(c * chunk + i * BASE_TILE, BASE_TILE), BASE_TILE)
            product = jnp.dot(att[...], w[:, cols], preferred_element_type=F32).astype(BF16)
            for to in range(tensors):
                part[to, :, cols] = product[to * rows_dev:(to + 1) * rows_dev]

    for c in range(EARLY):
        compute_base(c)

    pl.semaphore_wait(barrier, owners - 1 + tensors - 1)

    def send_rows(j, k):
        mine, cols = pl.ds(j * capacity, capacity), pl.ds(k * strip, strip)
        return pltpu.make_async_remote_copy(
            src_ref=slots.at[mine, cols], dst_ref=got.at[mine, cols],
            send_sem=rows_send.at[j - 1, k], recv_sem=rows_recv.at[j - 1, k],
            device_id={"adapter": lax.rem(me + j, owners)}, device_id_type=MESH,
        )

    def send_ids(j):
        mine = pl.ds(j * capacity, capacity)
        return pltpu.make_async_remote_copy(
            src_ref=slot_ids.at[mine], dst_ref=got_ids.at[mine],
            send_sem=ids_send.at[j - 1], recv_sem=ids_recv.at[j - 1],
            device_id={"adapter": lax.rem(me + j, owners)}, device_id_type=MESH,
        )

    def send_pair(i, c):
        cols = pl.ds(c * chunk, chunk)
        return pltpu.make_async_remote_copy(
            src_ref=part.at[partner_across if i else partner, :, cols], dst_ref=pair_in.at[i, :, cols],
            send_sem=pair_send.at[i, c], recv_sem=pair_recv.at[i, c],
            device_id={"tensor": partner}, device_id_type=MESH,
        )

    def send_cross(c):
        cols = pl.ds(c * chunk, chunk)
        return pltpu.make_async_remote_copy(
            src_ref=cross.at[:, cols], dst_ref=cross_in.at[:, cols],
            send_sem=cross_send.at[c], recv_sem=cross_recv.at[c],
            device_id={"tensor": across}, device_id_type=MESH,
        )

    def send_low(j):
        return pltpu.make_async_remote_copy(
            src_ref=low, dst_ref=low_in.at[j - 1],
            send_sem=low_send.at[j - 1], recv_sem=low_recv.at[j - 1],
            device_id={"tensor": lax.rem(plane + j, tensors)}, device_id_type=MESH,
        )

    def send_corr(j, c):
        mine, cols = pl.ds(j * capacity, capacity), pl.ds(c * piece, piece)
        return pltpu.make_async_remote_copy(
            src_ref=corr.at[mine, cols], dst_ref=ret.at[mine, cols],
            send_sem=corr_send.at[j - 1, c], recv_sem=corr_recv.at[j - 1, c],
            device_id={"adapter": lax.rem(me - j + owners, owners)}, device_id_type=MESH,
        )

    def send_home(j, c):
        cols = pl.ds(c * piece, piece)
        to = lax.rem(plane + j, tensors)
        return pltpu.make_async_remote_copy(
            src_ref=home.at[to, :, cols], dst_ref=home_in.at[j - 1, :, cols],
            send_sem=home_send.at[j - 1, c], recv_sem=home_recv.at[j - 1, c],
            device_id={"tensor": to}, device_id_type=MESH,
        )

    def send_base(c):
        send_pair(1, c).start()
        send_pair(0, c).start()

    def base(c):
        if c + 2 < base_chunks:
            load_w(c + 2).start()
        compute_base(c)
        send_base(c)

    def forward(c):
        send_pair(1, c).wait_recv()
        cols = pl.ds(c * chunk, chunk)
        cross[:, cols] = (part[across, :, cols].astype(F32) + pair_in[1, :, cols].astype(F32)).astype(BF16)
        send_cross(c).start()

    lane_parity = lax.div(lax.broadcasted_iota(jnp.int32, (n_slots, lanes), 1), rank)

    def shrink(k, total):
        load_s(k).wait()
        for j in range(1, owners):
            send_rows(j, k).wait_recv()
        wanted = got_ids[...] - lane_parity

        def step(i, total):
            some = pl.ds(pl.multiple_of(i * WIDE, WIDE), WIDE)
            products = lax.dot_general(
                got[:, k * strip:(k + 1) * strip], s[some, k * strip:(k + 1) * strip],
                (((1,), (1,)), ((), ())), preferred_element_type=F32,
            )
            for p in range(WIDE // lanes):
                here = products[:, p * lanes:(p + 1) * lanes]
                total += jnp.where(wanted == 2 * (i * (WIDE // lanes) + p), here, 0.0)
            return total

        return lax.fori_loop(0, low_width // WIDE, step, total)

    def send_total(total):
        both = total + pltpu.roll(total, rank, 1)
        packed = jnp.where(lane_parity[:n_slots // 2] == 0, both[:n_slots // 2], both[n_slots // 2:])
        low[...] = packed.astype(BF16)
        for j in range(1, tensors):
            send_low(j).start()

    def expand():
        packed = low[...].astype(F32)
        for j in range(1, tensors):
            send_low(j).wait_recv()
            packed += low_in[j - 1].astype(F32)
        turned = pltpu.roll(packed, rank, 1)
        first = lane_parity[:n_slots // 2] == 0
        shrunk = jnp.concatenate([jnp.where(first, packed, turned), jnp.where(first, turned, packed)], axis=0)
        wanted = got_ids[...] - lane_parity
        for p in range(low_width // lanes):
            spread[:, p * lanes:(p + 1) * lanes] = jnp.where(wanted == 2 * p, shrunk, 0.0).astype(BF16)
        for c in range(expand_chunks):
            load_e(c).wait()

            @pl.loop(0, 1)
            def _(i):
                cols = pl.ds(c * piece, piece)
                corr[:, cols] = (
                    ADAPTER_SCALING * jnp.dot(spread[...], e[:, cols], preferred_element_type=F32)
                ).astype(BF16)

            for j in range(1, owners):
                send_corr(j, c).start()
        ret[pl.ds(0, capacity)] = corr[pl.ds(0, capacity)]

    def merge(c):
        for j in range(1, owners):
            send_corr(j, c).wait_recv()
        cols = pl.ds(c * piece, piece)
        merged = jnp.dot(home_hot[...], ret[:, cols], preferred_element_type=F32).astype(BF16)
        for to in range(tensors):
            home[to, :, cols] = merged[to * rows_dev:(to + 1) * rows_dev]
        for j in range(1, tensors):
            send_home(j, c).start()

    for j in range(1, owners):
        send_ids(j).start()
    for k in range(row_chunks):
        for j in range(1, owners):
            send_rows(j, k).start()
    got[pl.ds(0, capacity)] = slots[pl.ds(0, capacity)]
    got_ids[pl.ds(0, capacity)] = slot_ids[pl.ds(0, capacity)]
    for c in range(expand_chunks):
        load_e(c).start()
    base(0)
    base(1)
    base(2)
    base(3)
    forward(0)
    for j in range(1, owners):
        send_ids(j).wait_recv()
    total = jnp.zeros((n_slots, lanes), F32)
    for k in range(row_chunks):
        total = shrink(k, total)
    send_total(total)
    forward(1)
    base(4)
    base(5)
    base(6)
    forward(2)
    expand()
    base(7)
    forward(3)
    forward(4)
    forward(5)
    merge(0)
    forward(6)
    merge(1)
    forward(7)
    merge(2)
    merge(3)

    for c in range(base_chunks):
        cols = pl.ds(c * chunk, chunk)
        send_pair(0, c).wait_recv()
        send_cross(c).wait_recv()
        total = part[plane, :, cols].astype(F32) + pair_in[0, :, cols].astype(F32)
        out_ref[:, cols] = total + cross_in[:, cols].astype(F32)
    for j in range(tensors):
        for c in range(expand_chunks):
            if j:
                send_home(j, c).wait_recv()
        source = lax.rem(plane - j + tensors, tensors)
        cols = pl.ds(pl.multiple_of(source * slice_width, slice_width), slice_width)
        own = home_in[j - 1] if j else home[plane]
        out_ref[:, cols] += own.astype(F32)

    for j in range(1, owners):
        send_ids(j).wait_send()
        for k in range(row_chunks):
            send_rows(j, k).wait_send()
        for c in range(expand_chunks):
            send_corr(j, c).wait_send()
    for j in range(1, tensors):
        send_low(j).wait_send()
        for c in range(expand_chunks):
            send_home(j, c).wait_send()
    for c in range(base_chunks):
        send_pair(0, c).wait_send()
        send_pair(1, c).wait_send()
        send_cross(c).wait_send()


def fused(attended, out_weight, adapter_ids, shrink_weight, expand_weight):
    owners, tensors = lax.axis_size("adapter"), lax.axis_size("tensor")
    rows, features = attended.shape[1:]
    width = out_weight.shape[1]
    adapters, rank, slice_width = expand_weight.shape
    low_width, lanes = adapters * rank, 2 * rank
    n_slots, rows_dev = owners * (rows // 2), rows // tensors
    base_chunks, expand_chunks, row_chunks = 8, 4, 1
    dma = lambda *shape: pltpu.SemaphoreType.DMA(shape)
    pairs = lambda n: [dma(n), dma(n)]
    grids = lambda n, m: [dma(n, m), dma(n, m)]
    vmem = lambda *shape: pltpu.VMEM(shape, BF16)
    ints = lambda *shape: pltpu.VMEM(shape, jnp.int32)
    summed = pl.pallas_call(
        functools.partial(fused_kernel, owners, tensors, base_chunks, expand_chunks, row_chunks),
        out_shape=jax.ShapeDtypeStruct((rows_dev, width), F32),
        in_specs=[pl.BlockSpec(memory_space=pltpu.VMEM)] + [pl.BlockSpec(memory_space=pl.ANY)] * 4,
        out_specs=pl.BlockSpec(memory_space=pltpu.VMEM),
        scratch_shapes=[
            vmem(rows, features),
            vmem(features, width),
            vmem(low_width, features),
            vmem(low_width, slice_width),
            vmem(n_slots, features),
            ints(n_slots, lanes),
            vmem(n_slots, features),
            ints(n_slots, lanes),
            vmem(rows, n_slots),
            vmem(tensors, rows_dev, width),
            vmem(2, rows_dev, width),
            vmem(rows_dev, width),
            vmem(rows_dev, width),
            vmem(n_slots // 2, lanes),
            vmem(tensors - 1, n_slots // 2, lanes),
            vmem(n_slots, low_width),
            vmem(n_slots, slice_width),
            vmem(n_slots, slice_width),
            vmem(tensors, rows_dev, slice_width),
            vmem(tensors - 1, rows_dev, slice_width),
            pltpu.SemaphoreType.DMA,
            dma(base_chunks),
            dma(row_chunks),
            dma(expand_chunks),
            *grids(owners - 1, row_chunks),
            *pairs(owners - 1),
            *pairs(tensors - 1),
            *grids(2, base_chunks),
            *pairs(base_chunks),
            *grids(owners - 1, expand_chunks),
            *grids(tensors - 1, expand_chunks),
        ],
        compiler_params=pltpu.CompilerParams(
            collective_id=0, has_side_effects=True, vmem_limit_bytes=VMEM_LIMIT
        ),
    )(
        adapter_ids,
        attended[0],
        out_weight,
        jnp.swapaxes(shrink_weight, 1, 2).reshape(low_width, features),
        expand_weight.reshape(low_width, slice_width),
    )
    return summed.astype(BF16)[None]


def fits(attended, out_weight, shrink_weight, expand_weight):
    owners, tensors = lax.axis_size("adapter"), lax.axis_size("tensor")
    rows, features = attended.shape[1:]
    width, slice_width = out_weight.shape[1], expand_weight.shape[2]
    low_width = expand_weight.shape[0] * expand_weight.shape[1]
    slots = owners * (rows // 2)
    values = out_weight.size + shrink_weight.size + expand_weight.size
    values += rows * (features + 4 * width) + slots * (2 * features + low_width + 3 * slice_width)
    tiled = rows % (16 * tensors) == 0 and width % (8 * TILE) == 0 and slice_width % (4 * TILE) == 0
    tiled = tiled and tensors == 4 and features % (4 * TILE) == 0 and low_width % WIDE == 0
    return tiled and 2 * values <= VMEM_LIMIT


def plain(attended, out_weight, adapter_ids, shrink_weight, expand_weight):
    inputs = attended[0]
    rows_all, features = inputs.shape
    owners = lax.axis_size("adapter")
    adapters_dev = shrink_weight.shape[0]
    capacity = rows_all // 2
    row_ids = adapter_ids[0]
    owning_adapter = row_ids // adapters_dev
    local_slot = row_ids % adapters_dev
    owner_hot = (owning_adapter[:, None] == jnp.arange(owners)[None, :]).astype(jnp.int32)
    running = jnp.cumsum(owner_hot, axis=0) - 1
    slot_of = owning_adapter * capacity + jnp.sum(running * owner_hot, axis=1)
    slot_ids = jnp.full((owners * capacity,), -1, jnp.int32).at[slot_of].set(local_slot)
    outgoing = jnp.zeros((owners * capacity, features), jnp.bfloat16).at[slot_of].set(inputs)
    recv_rows, recv_ids = (
        lax.all_to_all(outgoing, "adapter", split_axis=0, concat_axis=0, tiled=True),
        lax.all_to_all(slot_ids, "adapter", split_axis=0, concat_axis=0, tiled=True),
    )
    chosen = (recv_ids[:, None] == jnp.arange(adapters_dev)[None, :]).astype(jnp.float32)
    products = jnp.einsum(
        "nd,adr->nar", recv_rows, shrink_weight, preferred_element_type=jnp.float32
    )
    partial_sum = jnp.sum(products * chosen[:, :, None], axis=1)
    incoming_rows = lax.psum(partial_sum.astype(jnp.bfloat16), "tensor")
    spread = incoming_rows[:, None, :] * chosen.astype(jnp.bfloat16)[:, :, None]
    delta_rows = (
        ADAPTER_SCALING
        * jnp.einsum("nar,ard->nd", spread, expand_weight, preferred_element_type=jnp.float32)
    ).astype(jnp.bfloat16)
    returned = lax.all_to_all(delta_rows, "adapter", split_axis=0, concat_axis=0, tiled=True)
    home_delta = returned[slot_of]
    summed = lax.psum_scatter(
        jnp.dot(inputs, out_weight, preferred_element_type=jnp.float32).astype(jnp.bfloat16),
        "tensor",
        scatter_dimension=0,
        tiled=True,
    ).astype(jnp.float32)
    own_delta = lax.all_to_all(home_delta, "tensor", split_axis=0, concat_axis=1, tiled=True)
    projected = (summed + own_delta.astype(jnp.float32)).astype(jnp.bfloat16)
    return projected[None]


def per_device(attended, out_weight, adapter_ids, shrink_weight, expand_weight):
    form = fused if fits(attended, out_weight, shrink_weight, expand_weight) else plain
    return form(attended, out_weight, adapter_ids, shrink_weight, expand_weight)


def solution(mesh):
    return jax.shard_map(
        per_device,
        mesh=mesh,
        in_specs=(
            P(("groups", "adapter"), None, "tensor"),
            P("tensor", None),
            P(("groups", "adapter"), None),
            P("adapter", "tensor", None),
            P("adapter", None, "tensor"),
        ),
        out_specs=P(("groups", "adapter"), "tensor", None),
        check_vma=False,
    )
```

```python
import functools

import jax
import jax.numpy as jnp
from jax import lax
from jax.experimental import pallas as pl
from jax.experimental.pallas import tpu as pltpu
from jax.sharding import PartitionSpec as P

ADAPTER_SCALING = 0.5
MESH = pl.DeviceIdType.MESH
TILE = 256
BASE_TILE = 512
WIDE = 2048
EARLY = 0
VMEM_LIMIT = 60 * 2**20
F32 = jnp.float32
BF16 = jnp.bfloat16


def fused_kernel(
    owners, tensors, base_chunks, expand_chunks, row_chunks,
    ids_ref, att_hbm, w_hbm, s_hbm, e_hbm, out_ref,
    att, w, s, e, slots, slot_ids, got, got_ids, home_hot,
    part, pair_in, cross, cross_in, low, low_in, spread, corr, ret, home, home_in,
    att_sem, w_sem, s_sem, e_sem,
    rows_send, rows_recv, ids_send, ids_recv, low_send, low_recv,
    pair_send, pair_recv, cross_send, cross_recv, corr_send, corr_recv, home_send, home_recv,
):
    rows, features = att.shape
    width = w.shape[1]
    low_width, slice_width = e.shape
    lanes = slot_ids.shape[1]
    capacity = rows // 2
    n_slots = owners * capacity
    rows_dev = rows // tensors
    rank = lanes // 2
    adapters = low_width // rank
    chunk = width // base_chunks
    piece = slice_width // expand_chunks
    strip = features // row_chunks
    me = lax.axis_index("adapter")
    plane = lax.axis_index("tensor")
    partner = plane + 1 - 2 * lax.rem(plane, 2)
    across = lax.rem(plane + 2, tensors)
    partner_across = lax.rem(partner + 2, tensors)

    def load_w(c):
        cols = pl.ds(c * chunk, chunk)
        return pltpu.make_async_copy(w_hbm.at[:, cols], w.at[:, cols], w_sem.at[c])

    def load_s(k):
        cols = pl.ds(k * strip, strip)
        return pltpu.make_async_copy(s_hbm.at[:, cols], s.at[:, cols], s_sem.at[k])

    def load_e(c):
        cols = pl.ds(c * piece, piece)
        return pltpu.make_async_copy(e_hbm.at[:, cols], e.at[:, cols], e_sem.at[c])

    load_att = pltpu.make_async_copy(att_hbm, att, att_sem)
    load_att.start()
    for c in range(EARLY):
        load_w(c).start()
    for k in range(row_chunks):
        load_s(k).start()
    for c in range(EARLY, EARLY + 2):
        load_w(c).start()

    barrier = pltpu.get_barrier_semaphore()
    for j in range(1, owners):
        pl.semaphore_signal(barrier, inc=1, device_id={"adapter": lax.rem(me + j, owners)}, device_id_type=MESH)
    for j in range(1, tensors):
        pl.semaphore_signal(barrier, inc=1, device_id={"tensor": lax.rem(plane + j, tensors)}, device_id_type=MESH)

    ids = ids_ref[...]
    relative = lax.rem(lax.div(ids, adapters) - me + owners, owners)
    below = lax.broadcasted_iota(jnp.int32, (rows, rows), 0)
    along = lax.broadcasted_iota(jnp.int32, (rows, rows), 1)

    def as_column(row):
        return jnp.sum(jnp.where(below == along, row, 0), axis=1, keepdims=True)

    same = as_column(relative) == relative
    running = jnp.sum(jnp.where(same & (below < along), 1, 0), axis=0, keepdims=True)
    slot_of = relative * capacity + running
    hot = lax.broadcasted_iota(jnp.int32, (n_slots, rows), 0) == slot_of
    home_hot[...] = jnp.where(
        lax.broadcasted_iota(jnp.int32, (rows, n_slots), 1) == as_column(slot_of), 1.0, 0.0
    ).astype(BF16)
    local_slot = jnp.sum(jnp.where(hot, lax.rem(ids, adapters) + 1, 0), axis=1, keepdims=True) - 1
    slot_ids[...] = jnp.broadcast_to(local_slot, (n_slots, lanes))
    load_att.wait()
    hot = jnp.where(hot, 1.0, 0.0).astype(BF16)

    @pl.loop(0, features // TILE)
    def _(i):
        cols = pl.ds(pl.multiple_of(i * TILE, TILE), TILE)
        slots[:, cols] = jnp.dot(hot, att[:, cols], preferred_element_type=F32).astype(BF16)

    def compute_base(c):
        load_w(c).wait()

        @pl.loop(0, chunk // BASE_TILE)
        def _(i):
            cols = pl.ds(pl.multiple_of(c * chunk + i * BASE_TILE, BASE_TILE), BASE_TILE)
            product = jnp.dot(att[...], w[:, cols], preferred_element_type=F32).astype(BF16)
            for to in range(tensors):
                part[to, :, cols] = product[to * rows_dev:(to + 1) * rows_dev]

    for c in range(EARLY):
        compute_base(c)

    pl.semaphore_wait(barrier, owners - 1 + tensors - 1)

    def send_rows(j, k):
        mine, cols = pl.ds(j * capacity, capacity), pl.ds(k * strip, strip)
        return pltpu.make_async_remote_copy(
            src_ref=slots.at[mine, cols], dst_ref=got.at[mine, cols],
            send_sem=rows_send.at[j - 1, k], recv_sem=rows_recv.at[j - 1, k],
            device_id={"adapter": lax.rem(me + j, owners)}, device_id_type=MESH,
        )

    def send_ids(j):
        mine = pl.ds(j * capacity, capacity)
        return pltpu.make_async_remote_copy(
            src_ref=slot_ids.at[mine], dst_ref=got_ids.at[mine],
            send_sem=ids_send.at[j - 1], recv_sem=ids_recv.at[j - 1],
            device_id={"adapter": lax.rem(me + j, owners)}, device_id_type=MESH,
        )

    def send_pair(i, c):
        cols = pl.ds(c * chunk, chunk)
        return pltpu.make_async_remote_copy(
            src_ref=part.at[partner_across if i else partner, :, cols], dst_ref=pair_in.at[i, :, cols],
            send_sem=pair_send.at[i, c], recv_sem=pair_recv.at[i, c],
            device_id={"tensor": partner}, device_id_type=MESH,
        )

    def send_cross(c):
        cols = pl.ds(c * chunk, chunk)
        return pltpu.make_async_remote_copy(
            src_ref=cross.at[:, cols], dst_ref=cross_in.at[:, cols],
            send_sem=cross_send.at[c], recv_sem=cross_recv.at[c],
            device_id={"tensor": across}, device_id_type=MESH,
        )

    def send_low(j):
        return pltpu.make_async_remote_copy(
            src_ref=low, dst_ref=low_in.at[j - 1],
            send_sem=low_send.at[j - 1], recv_sem=low_recv.at[j - 1],
            device_id={"tensor": lax.rem(plane + j, tensors)}, device_id_type=MESH,
        )

    def send_corr(j, c):
        mine, cols = pl.ds(j * capacity, capacity), pl.ds(c * piece, piece)
        return pltpu.make_async_remote_copy(
            src_ref=corr.at[mine, cols], dst_ref=ret.at[mine, cols],
            send_sem=corr_send.at[j - 1, c], recv_sem=corr_recv.at[j - 1, c],
            device_id={"adapter": lax.rem(me - j + owners, owners)}, device_id_type=MESH,
        )

    def send_home(j, c):
        cols = pl.ds(c * piece, piece)
        to = lax.rem(plane + j, tensors)
        return pltpu.make_async_remote_copy(
            src_ref=home.at[to, :, cols], dst_ref=home_in.at[j - 1, :, cols],
            send_sem=home_send.at[j - 1, c], recv_sem=home_recv.at[j - 1, c],
            device_id={"tensor": to}, device_id_type=MESH,
        )

    def send_base(c):
        send_pair(1, c).start()
        send_pair(0, c).start()

    def base(c):
        if c + 2 < base_chunks:
            load_w(c + 2).start()
        compute_base(c)
        send_base(c)

    def forward(c):
        send_pair(1, c).wait_recv()
        cols = pl.ds(c * chunk, chunk)
        cross[:, cols] = (part[across, :, cols].astype(F32) + pair_in[1, :, cols].astype(F32)).astype(BF16)
        send_cross(c).start()

    lane_parity = lax.div(lax.broadcasted_iota(jnp.int32, (n_slots, lanes), 1), rank)

    def shrink(k, total):
        load_s(k).wait()
        for j in range(1, owners):
            send_rows(j, k).wait_recv()
        wanted = got_ids[...] - lane_parity

        def step(i, total):
            some = pl.ds(pl.multiple_of(i * WIDE, WIDE), WIDE)
            products = lax.dot_general(
                got[:, k * strip:(k + 1) * strip], s[some, k * strip:(k + 1) * strip],
                (((1,), (1,)), ((), ())), preferred_element_type=F32,
            )
            for p in range(WIDE // lanes):
                here = products[:, p * lanes:(p + 1) * lanes]
                total += jnp.where(wanted == 2 * (i * (WIDE // lanes) + p), here, 0.0)
            return total

        return lax.fori_loop(0, low_width // WIDE, step, total)

    def send_total(total):
        both = total + pltpu.roll(total, rank, 1)
        packed = jnp.where(lane_parity[:n_slots // 2] == 0, both[:n_slots // 2], both[n_slots // 2:])
        low[...] = packed.astype(BF16)
        for j in range(1, tensors):
            send_low(j).start()

    def expand():
        packed = low[...].astype(F32)
        for j in range(1, tensors):
            send_low(j).wait_recv()
            packed += low_in[j - 1].astype(F32)
        turned = pltpu.roll(packed, rank, 1)
        first = lane_parity[:n_slots // 2] == 0
        shrunk = jnp.concatenate([jnp.where(first, packed, turned), jnp.where(first, turned, packed)], axis=0)
        wanted = got_ids[...] - lane_parity
        for p in range(low_width // lanes):
            spread[:, p * lanes:(p + 1) * lanes] = jnp.where(wanted == 2 * p, shrunk, 0.0).astype(BF16)
        for c in range(expand_chunks):
            load_e(c).wait()

            @pl.loop(0, 1)
            def _(i):
                cols = pl.ds(c * piece, piece)
                corr[:, cols] = (
                    ADAPTER_SCALING * jnp.dot(spread[...], e[:, cols], preferred_element_type=F32)
                ).astype(BF16)

            for j in range(1, owners):
                send_corr(j, c).start()
        ret[pl.ds(0, capacity)] = corr[pl.ds(0, capacity)]

    def merge(c):
        for j in range(1, owners):
            send_corr(j, c).wait_recv()
        cols = pl.ds(c * piece, piece)
        merged = jnp.dot(home_hot[...], ret[:, cols], preferred_element_type=F32).astype(BF16)
        for to in range(tensors):
            home[to, :, cols] = merged[to * rows_dev:(to + 1) * rows_dev]
        for j in range(1, tensors):
            send_home(j, c).start()

    for j in range(1, owners):
        send_ids(j).start()
    for k in range(row_chunks):
        for j in range(1, owners):
            send_rows(j, k).start()
    got[pl.ds(0, capacity)] = slots[pl.ds(0, capacity)]
    got_ids[pl.ds(0, capacity)] = slot_ids[pl.ds(0, capacity)]
    for c in range(expand_chunks):
        load_e(c).start()
    base(0)
    base(1)
    for j in range(1, owners):
        send_ids(j).wait_recv()
    total = jnp.zeros((n_slots, lanes), F32)
    for k in range(row_chunks):
        total = shrink(k, total)
    send_total(total)
    forward(0)
    base(2)
    base(3)
    expand()
    forward(1)
    forward(2)
    merge(0)
    forward(3)
    merge(1)

    for c in range(base_chunks):
        cols = pl.ds(c * chunk, chunk)
        send_pair(0, c).wait_recv()
        send_cross(c).wait_recv()
        total = part[plane, :, cols].astype(F32) + pair_in[0, :, cols].astype(F32)
        out_ref[:, cols] = total + cross_in[:, cols].astype(F32)
    for j in range(tensors):
        for c in range(expand_chunks):
            if j:
                send_home(j, c).wait_recv()
        source = lax.rem(plane - j + tensors, tensors)
        cols = pl.ds(pl.multiple_of(source * slice_width, slice_width), slice_width)
        own = home_in[j - 1] if j else home[plane]
        out_ref[:, cols] += own.astype(F32)

    for j in range(1, owners):
        send_ids(j).wait_send()
        for k in range(row_chunks):
            send_rows(j, k).wait_send()
        for c in range(expand_chunks):
            send_corr(j, c).wait_send()
    for j in range(1, tensors):
        send_low(j).wait_send()
        for c in range(expand_chunks):
            send_home(j, c).wait_send()
    for c in range(base_chunks):
        send_pair(0, c).wait_send()
        send_pair(1, c).wait_send()
        send_cross(c).wait_send()


def fused(attended, out_weight, adapter_ids, shrink_weight, expand_weight):
    owners, tensors = lax.axis_size("adapter"), lax.axis_size("tensor")
    rows, features = attended.shape[1:]
    width = out_weight.shape[1]
    adapters, rank, slice_width = expand_weight.shape
    low_width, lanes = adapters * rank, 2 * rank
    n_slots, rows_dev = owners * (rows // 2), rows // tensors
    base_chunks, expand_chunks, row_chunks = 4, 2, 1
    dma = lambda *shape: pltpu.SemaphoreType.DMA(shape)
    pairs = lambda n: [dma(n), dma(n)]
    grids = lambda n, m: [dma(n, m), dma(n, m)]
    vmem = lambda *shape: pltpu.VMEM(shape, BF16)
    ints = lambda *shape: pltpu.VMEM(shape, jnp.int32)
    summed = pl.pallas_call(
        functools.partial(fused_kernel, owners, tensors, base_chunks, expand_chunks, row_chunks),
        out_shape=jax.ShapeDtypeStruct((rows_dev, width), F32),
        in_specs=[pl.BlockSpec(memory_space=pltpu.VMEM)] + [pl.BlockSpec(memory_space=pl.ANY)] * 4,
        out_specs=pl.BlockSpec(memory_space=pltpu.VMEM),
        scratch_shapes=[
            vmem(rows, features),
            vmem(features, width),
            vmem(low_width, features),
            vmem(low_width, slice_width),
            vmem(n_slots, features),
            ints(n_slots, lanes),
            vmem(n_slots, features),
            ints(n_slots, lanes),
            vmem(rows, n_slots),
            vmem(tensors, rows_dev, width),
            vmem(2, rows_dev, width),
            vmem(rows_dev, width),
            vmem(rows_dev, width),
            vmem(n_slots // 2, lanes),
            vmem(tensors - 1, n_slots // 2, lanes),
            vmem(n_slots, low_width),
            vmem(n_slots, slice_width),
            vmem(n_slots, slice_width),
            vmem(tensors, rows_dev, slice_width),
            vmem(tensors - 1, rows_dev, slice_width),
            pltpu.SemaphoreType.DMA,
            dma(base_chunks),
            dma(row_chunks),
            dma(expand_chunks),
            *grids(owners - 1, row_chunks),
            *pairs(owners - 1),
            *pairs(tensors - 1),
            *grids(2, base_chunks),
            *pairs(base_chunks),
            *grids(owners - 1, expand_chunks),
            *grids(tensors - 1, expand_chunks),
        ],
        compiler_params=pltpu.CompilerParams(
            collective_id=0, has_side_effects=True, vmem_limit_bytes=VMEM_LIMIT
        ),
    )(
        adapter_ids,
        attended[0],
        out_weight,
        jnp.swapaxes(shrink_weight, 1, 2).reshape(low_width, features),
        expand_weight.reshape(low_width, slice_width),
    )
    return summed.astype(BF16)[None]


def fits(attended, out_weight, shrink_weight, expand_weight):
    owners, tensors = lax.axis_size("adapter"), lax.axis_size("tensor")
    rows, features = attended.shape[1:]
    width, slice_width = out_weight.shape[1], expand_weight.shape[2]
    low_width = expand_weight.shape[0] * expand_weight.shape[1]
    slots = owners * (rows // 2)
    values = out_weight.size + shrink_weight.size + expand_weight.size
    values += rows * (features + 4 * width) + slots * (2 * features + low_width + 3 * slice_width)
    tiled = rows % (16 * tensors) == 0 and width % (8 * TILE) == 0 and slice_width % (4 * TILE) == 0
    tiled = tiled and tensors == 4 and features % (4 * TILE) == 0 and low_width % WIDE == 0
    return tiled and 2 * values <= VMEM_LIMIT


def plain(attended, out_weight, adapter_ids, shrink_weight, expand_weight):
    inputs = attended[0]
    rows_all, features = inputs.shape
    owners = lax.axis_size("adapter")
    adapters_dev = shrink_weight.shape[0]
    capacity = rows_all // 2
    row_ids = adapter_ids[0]
    owning_adapter = row_ids // adapters_dev
    local_slot = row_ids % adapters_dev
    owner_hot = (owning_adapter[:, None] == jnp.arange(owners)[None, :]).astype(jnp.int32)
    running = jnp.cumsum(owner_hot, axis=0) - 1
    slot_of = owning_adapter * capacity + jnp.sum(running * owner_hot, axis=1)
    slot_ids = jnp.full((owners * capacity,), -1, jnp.int32).at[slot_of].set(local_slot)
    outgoing = jnp.zeros((owners * capacity, features), jnp.bfloat16).at[slot_of].set(inputs)
    recv_rows, recv_ids = (
        lax.all_to_all(outgoing, "adapter", split_axis=0, concat_axis=0, tiled=True),
        lax.all_to_all(slot_ids, "adapter", split_axis=0, concat_axis=0, tiled=True),
    )
    chosen = (recv_ids[:, None] == jnp.arange(adapters_dev)[None, :]).astype(jnp.float32)
    products = jnp.einsum(
        "nd,adr->nar", recv_rows, shrink_weight, preferred_element_type=jnp.float32
    )
    partial_sum = jnp.sum(products * chosen[:, :, None], axis=1)
    incoming_rows = lax.psum(partial_sum.astype(jnp.bfloat16), "tensor")
    spread = incoming_rows[:, None, :] * chosen.astype(jnp.bfloat16)[:, :, None]
    delta_rows = (
        ADAPTER_SCALING
        * jnp.einsum("nar,ard->nd", spread, expand_weight, preferred_element_type=jnp.float32)
    ).astype(jnp.bfloat16)
    returned = lax.all_to_all(delta_rows, "adapter", split_axis=0, concat_axis=0, tiled=True)
    home_delta = returned[slot_of]
    summed = lax.psum_scatter(
        jnp.dot(inputs, out_weight, preferred_element_type=jnp.float32).astype(jnp.bfloat16),
        "tensor",
        scatter_dimension=0,
        tiled=True,
    ).astype(jnp.float32)
    own_delta = lax.all_to_all(home_delta, "tensor", split_axis=0, concat_axis=1, tiled=True)
    projected = (summed + own_delta.astype(jnp.float32)).astype(jnp.bfloat16)
    return projected[None]


def per_device(attended, out_weight, adapter_ids, shrink_weight, expand_weight):
    form = fused if fits(attended, out_weight, shrink_weight, expand_weight) else plain
    return form(attended, out_weight, adapter_ids, shrink_weight, expand_weight)


def solution(mesh):
    return jax.shard_map(
        per_device,
        mesh=mesh,
        in_specs=(
            P(("groups", "adapter"), None, "tensor"),
            P("tensor", None),
            P(("groups", "adapter"), None),
            P("adapter", "tensor", None),
            P("adapter", None, "tensor"),
        ),
        out_specs=P(("groups", "adapter"), "tensor", None),
        check_vma=False,
    )
```
